32 devices in a mesh: ctx: 8 (over y, x, core), head: 4 (over z).
Axes of the slice: x: 2, y: 2, z: 4, core: 2. Of those that a mesh axis runs over, the one named last changes fastest.
Arguments:
- queries: bfloat16 [256, 16384], P('ctx', 'head'), may hold values from -512 to 512
- kv_cache: bfloat16 [2, 4096, 1024], P(None, 'ctx', 'head'), may hold values from -7 to 7
- fill_len: int32 [8], P('ctx'), may hold values from 64 to 512
- prompt_offset: int32 [1], replicated, may hold values from 2048 to 3840
Outputs:
- attended: bfloat16 [256, 16384], P(('ctx', 'head'))
The draws below stay inside these ranges and needn't reach their ends.
All inputs are finite; a program needn't handle non-finite values.
Results may differ from the reference program's by a relative error of at most 0.0045.
Values may be sent and summed in bfloat16 or wider, within the bound.
A program may use at most 192 MiB of HBM per device.

```python
import math
import jax
import jax.numpy as jnp
from jax import lax

HEADS = 128
KV_HEADS = 8
HEAD_DIM = 128
SLOTS = 512
CACHE = 4096
PROMPT = 256
N_CTX = 8


def base_keys(key):
    normal_keys = jnp.clip(jax.random.normal(jax.random.fold_in(key, 11), (CACHE, KV_HEADS * HEAD_DIM), jnp.float32), -5.0, 5.0)
    row_scale = jnp.exp(jax.random.uniform(jax.random.fold_in(key, 13), (CACHE, 1), jnp.float32, math.log(0.7), math.log(1.4)))
    return normal_keys * row_scale


def draw_kv_cache(key, part):
    key_rows = base_keys(key)
    value_rows = jnp.clip(jax.random.normal(jax.random.fold_in(key, 12), (CACHE, KV_HEADS * HEAD_DIM), jnp.float32), -6.0, 6.0)
    return jnp.stack([key_rows, value_rows]).astype(jnp.bfloat16)


def draw_queries(key, part):
    shape_all = (PROMPT, HEADS * HEAD_DIM)
    drawn = jnp.clip(jax.random.normal(jax.random.fold_in(key, 21), shape_all, jnp.float32), -6.0, 6.0)
    drawn = drawn * jnp.exp(jax.random.uniform(jax.random.fold_in(key, 23), (PROMPT, 1), jnp.float32, 0.0, math.log(6.0)))
    return jnp.clip(drawn, -512.0, 512.0).astype(jnp.bfloat16)


def touch_ends(entries, own_key, low, high):
    place = [jax.random.randint(jax.random.fold_in(own_key, axis), (), 0, length) for axis, length in enumerate(entries.shape)]
    widest = entries.shape.index(max(entries.shape))
    beside = place[:widest] + [(place[widest] + 1) % entries.shape[widest]] + place[widest + 1:]
    return entries.at[tuple(place)].set(low).at[tuple(beside)].set(high)


def setup_inputs(seed: int = 0) -> dict:
    arg_keys = jax.random.split(jax.random.key(seed), 5)
    queries = draw_queries(jax.random.fold_in(arg_keys[4], 71), 0)
    kv_cache = draw_kv_cache(jax.random.fold_in(arg_keys[4], 71), 0)
    fill_len = touch_ends(jax.random.randint(arg_keys[2], (N_CTX,), SLOTS // 8, SLOTS + 1), jax.random.fold_in(arg_keys[2], 1), SLOTS // 8, SLOTS).astype(jnp.int32)
    prompt_offset = jax.random.randint(arg_keys[3], (1,), (N_CTX // 2) * SLOTS, CACHE - PROMPT + 1).astype(jnp.int32)
    return dict(queries=queries, kv_cache=kv_cache, fill_len=fill_len, prompt_offset=prompt_offset)


def ref_partial(query_groups, key_block, value_block, allowed):
    scaling = 1.0 / math.sqrt(HEAD_DIM)
    scores = jnp.einsum('nhgd,khd->hgnk', query_groups, key_block) * scaling
    scores = jnp.where(allowed[None, None], scores, -1e+30)
    row_max = lax.optimization_barrier(jnp.max(scores, axis=-1))
    weights = jnp.exp(scores - row_max[..., None])
    row_sum = lax.optimization_barrier(jnp.sum(weights, axis=-1))
    rounded = lax.optimization_barrier(weights.astype(jnp.bfloat16)).astype(jnp.float32)
    weighted = jnp.einsum('hgnk,khd->nhgd', rounded, value_block)
    weighted = weighted / jnp.transpose(row_sum, (2, 0, 1))[..., None]
    row_count = query_groups.shape[0]
    partial_value = lax.optimization_barrier(weighted.astype(jnp.bfloat16)).astype(jnp.float32)
    partial_value = partial_value.reshape(row_count, HEADS, HEAD_DIM)
    log_total = jnp.transpose(row_max + jnp.log(row_sum), (2, 0, 1)).reshape(row_count, HEADS)
    return (partial_value, log_total)

def reference(queries, kv_cache, fill_len, prompt_offset):
    groups = HEADS // KV_HEADS
    query_groups = queries.astype(jnp.float32).reshape(PROMPT, KV_HEADS, groups, HEAD_DIM)
    query_pos = prompt_offset[0] + jnp.arange(PROMPT, dtype=jnp.int32)
    key_shards = kv_cache[0].reshape(N_CTX, SLOTS, KV_HEADS, HEAD_DIM)
    value_shards = kv_cache[1].reshape(N_CTX, SLOTS, KV_HEADS, HEAD_DIM)
    slot_ids = jnp.arange(SLOTS, dtype=jnp.int32)

    def one_shard(running, inputs):
        key_block, value_block, shard_fill, shard_idx = inputs
        slot_pos = shard_idx * SLOTS + slot_ids
        allowed = (slot_ids < shard_fill)[None, :] & (slot_pos[None, :] <= query_pos[:, None])
        partial_value, log_total = ref_partial(query_groups, key_block.astype(jnp.float32), value_block.astype(jnp.float32), allowed)
        running_max, running_sum, running_acc = running
        new_max = jnp.maximum(running_max, log_total)
        old_scale = jnp.exp(running_max - new_max)
        new_scale = jnp.exp(log_total - new_max)
        return ((new_max, running_sum * old_scale + new_scale, running_acc * old_scale[..., None] + new_scale[..., None] * partial_value), None)
    initial = (jnp.full((PROMPT, HEADS), -1e+30, jnp.float32), jnp.zeros((PROMPT, HEADS), jnp.float32), jnp.zeros((PROMPT, HEADS, HEAD_DIM), jnp.float32))
    final_state, ignored = lax.scan(one_shard, initial, (key_shards, value_shards, fill_len, jnp.arange(N_CTX, dtype=jnp.int32)))
    final_max, final_sum, final_acc = final_state
    return (final_acc / final_sum[..., None]).reshape(PROMPT, HEADS * HEAD_DIM).astype(jnp.bfloat16)
```

```python
import functools
import math

import jax
import jax.numpy as jnp
from jax import lax
from jax.experimental import pallas as pl
from jax.experimental.pallas import tpu as pltpu
from jax.sharding import PartitionSpec as P

HEAD_DIM = 128
MESH = pl.DeviceIdType.MESH
FILL_ROWS = 16
NEG = -1e30


def xor(a, b, size):
    total = 0
    bit = 1
    while bit < size:
        total = total + lax.rem(lax.rem(lax.div(a, bit), 2) + lax.rem(lax.div(b, bit), 2), 2) * bit
        bit *= 2
    return total


def kernel(
    n_ctx, n_head, fill_ref, offset_ref, q_ref, kv_ref, out_ref,
    buf, other, qbuf, qt, acc, peak, total, staged, landed,
    local_sem, q_send, q_recv, kv_send, kv_recv, out_send, out_recv,
):
    ctx = lax.axis_index("ctx")
    head = lax.axis_index("head")
    core = lax.rem(ctx, 2)
    mate = 1 - core
    group = lax.div(ctx, 2)
    n_group = n_ctx // 2
    slots = kv_ref.shape[1]
    tokens = q_ref.shape[0]
    half = q_ref.shape[1] // 2
    heads = half // HEAD_DIM
    n_dest = 2 * n_head
    own_tokens = tokens // n_head
    block = own_tokens * heads
    rows = n_dest * block
    width = 2 * block
    scale = math.log2(math.e) / math.sqrt(HEAD_DIM)

    def columns(which, size):
        return pl.ds(pl.multiple_of(which * size, size), size)

    loads = []
    for index, (dst, which) in enumerate(((buf.at[core], core), (other, mate))):
        for part in range(2):
            loads.append(
                pltpu.make_async_copy(
                    kv_ref.at[part, :, columns(which, HEAD_DIM)],
                    dst.at[pl.ds(part * slots, slots)],
                    local_sem.at[2 * index + part],
                )
            )
    loads.append(
        pltpu.make_async_copy(q_ref.at[:, columns(core, half)], qbuf.at[core], local_sem.at[4])
    )
    for copy in loads:
        copy.start()
    fill = fill_ref[0]
    row_ids = lax.broadcasted_iota(jnp.int32, (FILL_ROWS, HEAD_DIM), 0)
    fill_rows = jnp.where(row_ids < 8, lax.div(fill, 8), lax.rem(fill, 8))
    fill_rows = fill_rows.astype(jnp.float32).astype(jnp.bfloat16)
    buf[core, pl.ds(2 * slots, FILL_ROWS)] = fill_rows
    other[pl.ds(2 * slots, FILL_ROWS)] = fill_rows

    barrier = pltpu.get_barrier_semaphore()

    @pl.loop(1, n_ctx)
    def _(step):
        pl.semaphore_signal(
            barrier, inc=1, device_id=(lax.rem(ctx + step, n_ctx), head), device_id_type=MESH
        )

    for step in range(1, n_head):
        for side in range(2):
            pl.semaphore_signal(
                barrier, inc=1, device_id=(2 * group + side, lax.rem(head + step, n_head)),
                device_id_type=MESH,
            )
    pl.semaphore_wait(barrier, n_ctx - 1 + 2 * (n_head - 1))

    q_copy = pltpu.make_async_remote_copy(
        src_ref=q_ref.at[:, columns(mate, half)], dst_ref=qbuf.at[core],
        send_sem=q_send, recv_sem=q_recv,
        device_id=(2 * group + mate, head), device_id_type=MESH,
    )
    q_copy.start()
    for copy in loads[:4]:
        copy.wait()

    def same(step):
        return pltpu.make_async_remote_copy(
            src_ref=buf.at[core], dst_ref=buf.at[core + 2 * step],
            send_sem=kv_send.at[2 * step], recv_sem=kv_recv.at[core + 2 * step],
            device_id=(2 * xor(group, step, n_group) + core, head), device_id_type=MESH,
        )

    def cross(step):
        return pltpu.make_async_remote_copy(
            src_ref=other, dst_ref=buf.at[core + 2 * step],
            send_sem=kv_send.at[2 * step + 1], recv_sem=kv_recv.at[core + 2 * step],
            device_id=(2 * xor(group, step, n_group) + mate, head), device_id_type=MESH,
        )

    cross(0).start()

    @pl.loop(1, n_group)
    def _(step):
        same(step).start()
        cross(step).start()

    loads[4].wait()
    q_copy.wait_recv()
    for dest in range(n_dest):
        side, part = dest // n_head, dest % n_head
        grown = qbuf[side].astype(jnp.float32)
        pieces = [
            grown[part * own_tokens:(part + 1) * own_tokens, i * HEAD_DIM:(i + 1) * HEAD_DIM]
            for i in range(heads)
        ]
        stacked = jnp.concatenate(pieces, axis=0)
        qt[:, dest * block:(dest + 1) * block] = jnp.transpose(stacked).astype(jnp.bfloat16)

    acc[...] = jnp.zeros_like(acc)
    total[...] = jnp.zeros_like(total)
    peak[...] = jnp.full_like(peak, NEG)

    offset = offset_ref[0]
    row = lax.broadcasted_iota(jnp.int32, (1, rows), 1)
    token = lax.div(row, block) * own_tokens + lax.rem(row, own_tokens)
    slot_ids = lax.broadcasted_iota(jnp.int32, (slots, width), 0)

    def chunk(index):
        shard = 2 * xor(group, lax.div(index, 2), n_group) + lax.rem(index, 2)
        keys = buf[index, pl.ds(0, slots)]
        values_t = jnp.transpose(buf[index, pl.ds(slots, slots)])
        info = buf[index, pl.ds(2 * slots, FILL_ROWS)].astype(jnp.float32)
        live = (info[0:1] * 8.0 + info[8:9]).astype(jnp.int32)
        live = jnp.concatenate([live] * (width // HEAD_DIM), axis=1)
        for start in range(0, rows, width):
            here = slice(start, start + width)
            position = offset + tokens * 2 * group + token[:, here] - shard * slots
            last = jnp.minimum(position, live - 1)
            scores = jnp.dot(keys, qt[:, here], preferred_element_type=jnp.float32)
            scores = jnp.where(slot_ids <= last, scores, NEG)
            old = peak[:, here]
            new = jnp.maximum(old, jnp.max(scores, axis=0, keepdims=True))
            fade = jnp.exp2((old - new) * scale)
            weights = jnp.exp2((scores - new) * scale)
            peak[:, here] = new
            total[:, here] = total[:, here] * fade + jnp.sum(weights, axis=0, keepdims=True)
            acc[:, here] = acc[:, here] * fade + jnp.dot(
                values_t, weights.astype(jnp.bfloat16), preferred_element_type=jnp.float32
            )

    def wait_slab(index):
        pltpu.make_async_copy(buf.at[index], buf.at[index], kv_recv.at[index]).wait()

    @pl.loop(0, n_ctx)
    def _(step):
        index = jnp.where(step < 2, lax.rem(core + step, 2), step)

        @pl.when(step > 0)
        def _():
            wait_slab(index)

        chunk(index)

    mine = core * n_head + head
    my_source = head * 2 + core

    def send(dest):
        return pltpu.make_async_remote_copy(
            src_ref=staged.at[dest], dst_ref=landed.at[my_source],
            send_sem=out_send.at[dest], recv_sem=out_recv.at[my_source],
            device_id=(2 * group + lax.div(dest, n_head), lax.rem(dest, n_head)),
            device_id_type=MESH,
        )

    def finished(dest):
        here = columns(dest, block)
        return jnp.transpose(acc[:, here] / total[:, here]).astype(jnp.bfloat16)

    @pl.loop(1, n_dest)
    def _(step):
        dest = lax.rem(mine + step, n_dest)
        staged[dest] = finished(dest)
        send(dest).start()

    landed[my_source] = finished(mine)

    @pl.loop(1, n_dest)
    def _(step):
        source = lax.rem(my_source + step, n_dest)
        pltpu.make_async_copy(landed.at[source], landed.at[source], out_recv.at[source]).wait()

    for source in range(n_dest):
        grown = landed[source].astype(jnp.float32)
        pieces = [grown[i * own_tokens:(i + 1) * own_tokens] for i in range(heads)]
        out_ref[:, source * half:(source + 1) * half] = jnp.concatenate(pieces, axis=1).astype(
            jnp.bfloat16
        )

    q_copy.wait_send()
    cross(0).wait_send()

    @pl.loop(1, n_group)
    def _(step):
        same(step).wait_send()
        cross(step).wait_send()

    @pl.loop(1, n_dest)
    def _(step):
        send(lax.rem(mine + step, n_dest)).wait_send()


def per_device(n_ctx, n_head, queries, kv_cache, fill_len, prompt_offset):
    tokens, feats = queries.shape
    slots = kv_cache.shape[1]
    half = feats // 2
    n_dest = 2 * n_head
    own_tokens = tokens // n_head
    block = own_tokens * (half // HEAD_DIM)
    rows = n_dest * block
    slab = 2 * slots + FILL_ROWS
    bf16, f32 = jnp.bfloat16, jnp.float32
    dma = pltpu.SemaphoreType.DMA
    return pl.pallas_call(
        functools.partial(kernel, n_ctx, n_head),
        out_shape=jax.ShapeDtypeStruct((own_tokens, n_head * feats), bf16),
        in_specs=[
            pl.BlockSpec(memory_space=pltpu.SMEM),
            pl.BlockSpec(memory_space=pltpu.SMEM),
            pl.BlockSpec(memory_space=pl.ANY),
            pl.BlockSpec(memory_space=pl.ANY),
        ],
        out_specs=pl.BlockSpec(memory_space=pltpu.VMEM),
        scratch_shapes=[
            pltpu.VMEM((n_ctx, slab, HEAD_DIM), bf16),
            pltpu.VMEM((slab, HEAD_DIM), bf16),
            pltpu.VMEM((2, tokens, half), bf16),
            pltpu.VMEM((HEAD_DIM, rows), bf16),
            pltpu.VMEM((HEAD_DIM, rows), f32),
            pltpu.VMEM((1, rows), f32),
            pltpu.VMEM((1, rows), f32),
            pltpu.VMEM((n_dest, block, HEAD_DIM), bf16),
            pltpu.VMEM((n_dest, block, HEAD_DIM), bf16),
            dma((5,)), dma, dma, dma((n_ctx,)), dma((n_ctx,)), dma((n_dest,)), dma((n_dest,)),
        ],
        compiler_params=pltpu.CompilerParams(
            collective_id=0, has_side_effects=True, vmem_limit_bytes=48 * 2**20
        ),
    )(fill_len, prompt_offset, queries, kv_cache)


def solution(mesh):
    in_specs = (P("ctx", "head"), P(None, "ctx", "head"), P("ctx"), P())
    out_specs = P(("ctx", "head"), None)
    return jax.shard_map(
        functools.partial(per_device, mesh.shape["ctx"], mesh.shape["head"]),
        mesh=mesh, in_specs=in_specs, out_specs=out_specs, check_vma=False,
    )
```

```python
import functools
import math

import jax
import jax.numpy as jnp
from jax import lax
from jax.experimental import pallas as pl
from jax.experimental.pallas import tpu as pltpu
from jax.sharding import PartitionSpec as P

HEAD_DIM = 128
MESH = pl.DeviceIdType.MESH
FILL_ROWS = 16
NEG = -1e30


def xor(a, b, size):
    total = 0
    bit = 1
    while bit < size:
        total = total + lax.rem(lax.rem(lax.div(a, bit), 2) + lax.rem(lax.div(b, bit), 2), 2) * bit
        bit *= 2
    return total


def kernel(
    n_ctx, n_head, fill_ref, offset_ref, q_ref, kv_ref, out_ref,
    buf, other, qbuf, qt, acc, peak, total, staged, landed,
    local_sem, q_send, q_recv, kv_send, kv_recv, out_send, out_recv,
):
    ctx = lax.axis_index("ctx")
    head = lax.axis_index("head")
    core = lax.rem(ctx, 2)
    mate = 1 - core
    group = lax.div(ctx, 2)
    n_group = n_ctx // 2
    slots = kv_ref.shape[1]
    tokens = q_ref.shape[0]
    half = q_ref.shape[1] // 2
    heads = half // HEAD_DIM
    n_dest = 2 * n_head
    own_tokens = tokens // n_head
    block = own_tokens * heads
    rows = n_dest * block
    width = 2 * block
    pack = 16 // own_tokens
    scale = math.log2(math.e) / math.sqrt(HEAD_DIM)

    def columns(which, size):
        return pl.ds(pl.multiple_of(which * size, size), size)

    loads = []
    for index, (dst, which) in enumerate(((buf.at[core], core), (other, mate))):
        for part in range(2):
            loads.append(
                pltpu.make_async_copy(
                    kv_ref.at[part, :, columns(which, HEAD_DIM)],
                    dst.at[pl.ds(part * slots, slots)],
                    local_sem.at[2 * index + part],
                )
            )
    loads.append(
        pltpu.make_async_copy(q_ref.at[:, columns(core, half)], qbuf.at[core], local_sem.at[4])
    )
    for copy in loads:
        copy.start()
    fill = fill_ref[0]
    row_ids = lax.broadcasted_iota(jnp.int32, (FILL_ROWS, HEAD_DIM), 0)
    fill_rows = jnp.where(row_ids < 8, lax.div(fill, 8), lax.rem(fill, 8))
    fill_rows = fill_rows.astype(jnp.float32).astype(jnp.bfloat16)
    buf[core, pl.ds(2 * slots, FILL_ROWS)] = fill_rows
    other[pl.ds(2 * slots, FILL_ROWS)] = fill_rows

    barrier = pltpu.get_barrier_semaphore()

    @pl.loop(1, n_ctx)
    def _(step):
        pl.semaphore_signal(
            barrier, inc=1, device_id=(lax.rem(ctx + step, n_ctx), head), device_id_type=MESH
        )

    for step in range(1, n_head):
        for side in range(2):
            pl.semaphore_signal(
                barrier, inc=1, device_id=(2 * group + side, lax.rem(head + step, n_head)),
                device_id_type=MESH,
            )

    def lay_out(side):
        for part in range(n_head):
            grown = qbuf[side, pl.ds(part // pack * 16, 16)].astype(jnp.float32)
            inner = part % pack * own_tokens
            pieces = [
                grown[inner:inner + own_tokens, i * HEAD_DIM:(i + 1) * HEAD_DIM]
                for i in range(heads)
            ]
            stacked = jnp.concatenate(pieces, axis=0)
            here = pl.ds(pl.multiple_of((side * n_head + part) * block, block), block)
            qt[:, here] = jnp.transpose(stacked).astype(jnp.bfloat16)

    loads[4].wait()
    lay_out(core)
    pl.semaphore_wait(barrier, n_ctx - 1 + 2 * (n_head - 1))

    q_copy = pltpu.make_async_remote_copy(
        src_ref=q_ref.at[:, columns(mate, half)], dst_ref=qbuf.at[core],
        send_sem=q_send, recv_sem=q_recv,
        device_id=(2 * group + mate, head), device_id_type=MESH,
    )
    q_copy.start()
    for copy in loads[:4]:
        copy.wait()

    def same(step):
        return pltpu.make_async_remote_copy(
            src_ref=buf.at[core], dst_ref=buf.at[core + 2 * step],
            send_sem=kv_send.at[2 * step], recv_sem=kv_recv.at[core + 2 * step],
            device_id=(2 * xor(group, step, n_group) + core, head), device_id_type=MESH,
        )

    def cross(step):
        return pltpu.make_async_remote_copy(
            src_ref=other, dst_ref=buf.at[core + 2 * step],
            send_sem=kv_send.at[2 * step + 1], recv_sem=kv_recv.at[core + 2 * step],
            device_id=(2 * xor(group, step, n_group) + mate, head), device_id_type=MESH,
        )

    cross(0).start()

    relayed = n_group == 4
    direct = 3 if relayed else n_group

    @pl.loop(1, direct)
    def _(turn):
        step = jnp.where(core == 0, direct - turn, turn) if relayed else turn
        same(step).start()
        cross(step).start()

    def relay(side):
        held = 2 * (2 - side) + side
        return pltpu.make_async_remote_copy(
            src_ref=buf.at[held], dst_ref=buf.at[6 + side],
            send_sem=kv_send.at[6 + side], recv_sem=kv_recv.at[6 + side],
            device_id=(2 * xor(group, 1 + side, n_group) + core, head), device_id_type=MESH,
        )

    q_copy.wait_recv()
    lay_out(mate)

    acc[...] = jnp.zeros_like(acc)
    total[...] = jnp.zeros_like(total)
    peak[...] = jnp.full_like(peak, NEG)

    offset = offset_ref[0]
    slot_ids = lax.broadcasted_iota(jnp.int32, (slots, width), 0)

    mine = core * n_head + head
    my_source = head * 2 + core

    def send(dest):
        return pltpu.make_async_remote_copy(
            src_ref=staged.at[dest], dst_ref=landed.at[my_source],
            send_sem=out_send.at[dest], recv_sem=out_recv.at[my_source],
            device_id=(2 * group + lax.div(dest, n_head), lax.rem(dest, n_head)),
            device_id_type=MESH,
        )

    def chunk(index, final):
        shard = 2 * xor(group, lax.div(index, 2), n_group) + lax.rem(index, 2)
        keys = buf[index, pl.ds(0, slots)]
        values_t = jnp.transpose(buf[index, pl.ds(slots, slots)])
        info = buf[index, pl.ds(2 * slots, FILL_ROWS)].astype(jnp.float32)
        live = (info[0:1] * 8.0 + info[8:9]).astype(jnp.int32)
        live = jnp.concatenate([live] * (width // HEAD_DIM), axis=1)
        pairs = n_head // 2
        for turn in range(2 * pairs):
            if final:
                pair = lax.rem(lax.div(head, 2) + 1 + turn // 2, pairs)
                place = turn % 2 * pairs + pair
                here = columns(place, width)
            else:
                place = turn
                here = slice(turn * width, (turn + 1) * width)
            row = place * width + lax.broadcasted_iota(jnp.int32, (1, width), 1)
            token = lax.div(row, block) * own_tokens + lax.rem(row, own_tokens)
            position = offset + tokens * 2 * group + token - shard * slots
            last = jnp.minimum(position, live - 1)
            scores = jnp.dot(keys, qt[:, here], preferred_element_type=jnp.float32)
            scores = jnp.where(slot_ids <= last, scores, NEG)
            old = peak[:, here]
            new = jnp.maximum(old, jnp.max(scores, axis=0, keepdims=True))
            fade = jnp.exp2((old - new) * scale)
            weights = jnp.exp2((scores - new) * scale)
            sums = total[:, here] * fade + jnp.sum(weights, axis=0, keepdims=True)
            out = acc[:, here] * fade + jnp.dot(
                values_t, weights.astype(jnp.bfloat16), preferred_element_type=jnp.float32
            )
            if not final:
                peak[:, here] = new
                total[:, here] = sums
                acc[:, here] = out
                continue
            done = jnp.transpose(out / sums).astype(jnp.bfloat16)
            for part in range(2):
                dest = 2 * place + part
                piece = done[part * block:(part + 1) * block]

                @pl.when(dest != mine)
                def _(dest=dest, piece=piece):
                    staged[dest] = piece
                    send(dest).start()

                @pl.when(dest == mine)
                def _(piece=piece):
                    landed[my_source] = piece

    def wait_slab(index):
        pltpu.make_async_copy(buf.at[index], buf.at[index], kv_recv.at[index]).wait()

    @pl.loop(0, n_ctx - 1)
    def _(step):
        index = jnp.where(step < 2, lax.rem(core + step, 2), step)
        waits = step > 0
        if relayed:
            index = jnp.where(step == 2, 3, jnp.where(step == 3, 4, jnp.where(step == 4, 2, index)))
            waits = (step == 1) | (step > 3)

            @pl.when(step == 2)
            def _():
                for side in range(2):
                    wait_slab(2 * (2 - side) + side)
                    relay(side).start()

        @pl.when(waits)
        def _():
            wait_slab(index)

        chunk(index, False)

    wait_slab(n_ctx - 1)
    chunk(n_ctx - 1, True)

    @pl.loop(1, n_dest)
    def _(step):
        source = lax.rem(my_source + step, n_dest)
        pltpu.make_async_copy(landed.at[source], landed.at[source], out_recv.at[source]).wait()

    for source in range(n_dest):
        grown = landed[source].astype(jnp.float32)
        pieces = [grown[i * own_tokens:(i + 1) * own_tokens] for i in range(heads)]
        out_ref[:, source * half:(source + 1) * half] = jnp.concatenate(pieces, axis=1).astype(
            jnp.bfloat16
        )

    q_copy.wait_send()
    cross(0).wait_send()

    @pl.loop(1, direct)
    def _(step):
        same(step).wait_send()
        cross(step).wait_send()

    if relayed:
        for side in range(2):
            relay(side).wait_send()

    @pl.loop(1, n_dest)
    def _(step):
        send(lax.rem(mine + step, n_dest)).wait_send()


def per_device(n_ctx, n_head, queries, kv_cache, fill_len, prompt_offset):
    tokens, feats = queries.shape
    slots = kv_cache.shape[1]
    half = feats // 2
    n_dest = 2 * n_head
    own_tokens = tokens // n_head
    block = own_tokens * (half // HEAD_DIM)
    rows = n_dest * block
    slab = 2 * slots + FILL_ROWS
    bf16, f32 = jnp.bfloat16, jnp.float32
    dma = pltpu.SemaphoreType.DMA
    return pl.pallas_call(
        functools.partial(kernel, n_ctx, n_head),
        out_shape=jax.ShapeDtypeStruct((own_tokens, n_head * feats), bf16),
        in_specs=[
            pl.BlockSpec(memory_space=pltpu.SMEM),
            pl.BlockSpec(memory_space=pltpu.SMEM),
            pl.BlockSpec(memory_space=pltpu.HBM),
            pl.BlockSpec(memory_space=pltpu.HBM),
        ],
        out_specs=pl.BlockSpec(memory_space=pltpu.VMEM),
        scratch_shapes=[
            pltpu.VMEM((n_ctx, slab, HEAD_DIM), bf16),
            pltpu.VMEM((slab, HEAD_DIM), bf16),
            pltpu.VMEM((2, tokens, half), bf16),
            pltpu.VMEM((HEAD_DIM, rows), bf16),
            pltpu.VMEM((HEAD_DIM, rows), f32),
            pltpu.VMEM((1, rows), f32),
            pltpu.VMEM((1, rows), f32),
            pltpu.VMEM((n_dest, block, HEAD_DIM), bf16),
            pltpu.VMEM((n_dest, block, HEAD_DIM), bf16),
            dma((5,)), dma, dma, dma((n_ctx,)), dma((n_ctx,)), dma((n_dest,)), dma((n_dest,)),
        ],
        compiler_params=pltpu.CompilerParams(
            collective_id=0, has_side_effects=True, vmem_limit_bytes=48 * 2**20
        ),
    )(fill_len, prompt_offset, queries, kv_cache)


def solution(mesh):
    in_specs = (P("ctx", "head"), P(None, "ctx", "head"), P("ctx"), P())
    out_specs = P(("ctx", "head"), None)
    return jax.shard_map(
        functools.partial(per_device, mesh.shape["ctx"], mesh.shape["head"]),
        mesh=mesh, in_specs=in_specs, out_specs=out_specs, check_vma=False,
    )
```

```python
import functools
import math

import jax
import jax.numpy as jnp
from jax import lax
from jax.experimental import pallas as pl
from jax.experimental.pallas import tpu as pltpu
from jax.sharding import PartitionSpec as P

HEAD_DIM = 128
MESH = pl.DeviceIdType.MESH
FILL_ROWS = 16
NEG = -1e30


def xor(a, b, size):
    total = 0
    bit = 1
    while bit < size:
        total = total + lax.rem(lax.rem(lax.div(a, bit), 2) + lax.rem(lax.div(b, bit), 2), 2) * bit
        bit *= 2
    return total


def kernel(
    n_ctx, n_head, fill_hbm, offset_hbm, q_ref, kv_ref, out_ref,
    buf, other, qbuf, qt, acc, peak, total, staged, landed,
    fill_ref, offset_ref, local_sem, q_send, q_recv, kv_send, kv_recv, out_send, out_recv,
):
    ctx = lax.axis_index("ctx")
    head = lax.axis_index("head")
    core = lax.rem(ctx, 2)
    mate = 1 - core
    group = lax.div(ctx, 2)
    n_group = n_ctx // 2
    slots = kv_ref.shape[1]
    tokens = q_ref.shape[0]
    half = q_ref.shape[1] // 2
    heads = half // HEAD_DIM
    n_dest = 2 * n_head
    own_tokens = tokens // n_head
    block = own_tokens * heads
    rows = n_dest * block
    pack = 16 // own_tokens
    scale = math.log2(math.e) / math.sqrt(HEAD_DIM)

    def columns(which, size):
        return pl.ds(pl.multiple_of(which * size, size), size)

    scalars = [
        pltpu.make_async_copy(fill_hbm, fill_ref, local_sem.at[5]),
        pltpu.make_async_copy(offset_hbm, offset_ref, local_sem.at[6]),
    ]
    for copy in scalars:
        copy.start()
    loads = []
    for index, (dst, which) in enumerate(((buf.at[core], core), (other, mate))):
        for part in range(2):
            loads.append(
                pltpu.make_async_copy(
                    kv_ref.at[part, :, columns(which, HEAD_DIM)],
                    dst.at[pl.ds(part * slots, slots)],
                    local_sem.at[2 * index + part],
                )
            )
    loads.append(
        pltpu.make_async_copy(q_ref.at[:, columns(core, half)], qbuf.at[core], local_sem.at[4])
    )
    for copy in loads:
        copy.start()
    barrier = pltpu.get_barrier_semaphore()

    @pl.loop(1, n_ctx)
    def _(step):
        pl.semaphore_signal(
            barrier, inc=1, device_id=(lax.rem(ctx + step, n_ctx), head), device_id_type=MESH
        )

    for step in range(1, n_head):
        for side in range(2):
            pl.semaphore_signal(
                barrier, inc=1, device_id=(2 * group + side, lax.rem(head + step, n_head)),
                device_id_type=MESH,
            )

    def lay_out(side):
        for part in range(n_head):
            grown = qbuf[side, pl.ds(part // pack * 16, 16)].astype(jnp.float32)
            inner = part % pack * own_tokens
            pieces = [
                grown[inner:inner + own_tokens, i * HEAD_DIM:(i + 1) * HEAD_DIM]
                for i in range(heads)
            ]
            stacked = jnp.concatenate(pieces, axis=0)
            here = pl.ds(pl.multiple_of((side * n_head + part) * block, block), block)
            qt[:, here] = jnp.transpose(stacked).astype(jnp.bfloat16)

    for copy in scalars:
        copy.wait()
    fill = fill_ref[0]
    row_ids = lax.broadcasted_iota(jnp.int32, (FILL_ROWS, HEAD_DIM), 0)
    fill_rows = jnp.where(row_ids < 8, lax.div(fill, 8), lax.rem(fill, 8))
    fill_rows = fill_rows.astype(jnp.float32).astype(jnp.bfloat16)
    buf[core, pl.ds(2 * slots, FILL_ROWS)] = fill_rows
    other[pl.ds(2 * slots, FILL_ROWS)] = fill_rows
    loads[4].wait()
    lay_out(core)
    pl.semaphore_wait(barrier, n_ctx - 1 + 2 * (n_head - 1))

    q_copy = pltpu.make_async_remote_copy(
        src_ref=q_ref.at[:, columns(mate, half)], dst_ref=qbuf.at[core],
        send_sem=q_send, recv_sem=q_recv,
        device_id=(2 * group + mate, head), device_id_type=MESH,
    )
    q_copy.start()
    for copy in loads[:4]:
        copy.wait()

    def same(step):
        return pltpu.make_async_remote_copy(
            src_ref=buf.at[core], dst_ref=buf.at[core + 2 * step],
            send_sem=kv_send.at[2 * step], recv_sem=kv_recv.at[core + 2 * step],
            device_id=(2 * xor(group, step, n_group) + core, head), device_id_type=MESH,
        )

    def cross(step):
        return pltpu.make_async_remote_copy(
            src_ref=other, dst_ref=buf.at[core + 2 * step],
            send_sem=kv_send.at[2 * step + 1], recv_sem=kv_recv.at[core + 2 * step],
            device_id=(2 * xor(group, step, n_group) + mate, head), device_id_type=MESH,
        )

    cross(0).start()

    relayed = n_group == 4
    direct = 3 if relayed else n_group

    @pl.loop(1, direct)
    def _(turn):
        step = jnp.where(core == 0, direct - turn, turn) if relayed else turn
        same(step).start()
        cross(step).start()

    def relay(side):
        held = 2 * (2 - side) + side
        return pltpu.make_async_remote_copy(
            src_ref=buf.at[held], dst_ref=buf.at[6 + side],
            send_sem=kv_send.at[6 + side], recv_sem=kv_recv.at[6 + side],
            device_id=(2 * xor(group, 1 + side, n_group) + core, head), device_id_type=MESH,
        )

    q_copy.wait_recv()
    lay_out(mate)

    acc[...] = jnp.zeros_like(acc)
    total[...] = jnp.zeros_like(total)
    peak[...] = jnp.full_like(peak, NEG)

    offset = offset_ref[0]

    mine = core * n_head + head
    my_source = head * 2 + core

    def send(dest):
        return pltpu.make_async_remote_copy(
            src_ref=staged.at[dest], dst_ref=landed.at[my_source],
            send_sem=out_send.at[dest], recv_sem=out_recv.at[my_source],
            device_id=(2 * group + lax.div(dest, n_head), lax.rem(dest, n_head)),
            device_id_type=MESH,
        )

    def chunk(index, final):
        shard = 2 * xor(group, lax.div(index, 2), n_group) + lax.rem(index, 2)
        keys = buf[index, pl.ds(0, slots)]
        values_t = jnp.transpose(buf[index, pl.ds(slots, slots)])
        info = buf[index, pl.ds(2 * slots, FILL_ROWS)].astype(jnp.float32)
        live = (info[0:1] * 8.0 + info[8:9]).astype(jnp.int32)
        pairs = n_head // 2
        width = 2 * block if final else rows
        live = jnp.concatenate([live] * (width // HEAD_DIM), axis=1)
        slot_ids = lax.broadcasted_iota(jnp.int32, (slots, width), 0)
        for turn in range(rows // width):
            if final:
                pair = lax.rem(lax.div(head, 2) + 1 + turn // 2, pairs)
                place = turn % 2 * pairs + pair
                here = columns(place, width)
            else:
                place = turn
                here = slice(turn * width, (turn + 1) * width)
            row = place * width + lax.broadcasted_iota(jnp.int32, (1, width), 1)
            token = lax.div(row, block) * own_tokens + lax.rem(row, own_tokens)
            position = offset + tokens * 2 * group + token - shard * slots
            last = jnp.minimum(position, live - 1)
            scores = jnp.dot(keys, qt[:, here], preferred_element_type=jnp.float32)
            scores = jnp.where(slot_ids <= last, scores, NEG)
            old = peak[:, here]
            new = jnp.maximum(old, jnp.max(scores, axis=0, keepdims=True))
            fade = jnp.exp2((old - new) * scale)
            weights = jnp.exp2((scores - new) * scale)
            sums = total[:, here] * fade + jnp.sum(weights, axis=0, keepdims=True)
            out = acc[:, here] * fade + jnp.dot(
                values_t, weights.astype(jnp.bfloat16), preferred_element_type=jnp.float32
            )
            if not final:
                peak[:, here] = new
                total[:, here] = sums
                acc[:, here] = out
                continue
            done = jnp.transpose(out / sums).astype(jnp.bfloat16)
            for part in range(2):
                dest = 2 * place + part
                piece = done[part * block:(part + 1) * block]

                @pl.when(dest != mine)
                def _(dest=dest, piece=piece):
                    staged[dest] = piece
                    send(dest).start()

                @pl.when(dest == mine)
                def _(piece=piece):
                    landed[my_source] = piece

    def wait_slab(index):
        pltpu.make_async_copy(buf.at[index], buf.at[index], kv_recv.at[index]).wait()

    @pl.loop(0, n_ctx - 1)
    def _(step):
        index = jnp.where(step < 2, lax.rem(core + step, 2), step)
        waits = step > 0
        if relayed:
            index = jnp.where(step == 2, 3, jnp.where(step == 3, 4, jnp.where(step == 4, 2, index)))
            waits = (step == 1) | (step > 3)

            @pl.when(step == 2)
            def _():
                for side in range(2):
                    wait_slab(2 * (2 - side) + side)
                    relay(side).start()

        @pl.when(waits)
        def _():
            wait_slab(index)

        chunk(index, False)

    wait_slab(n_ctx - 1)
    chunk(n_ctx - 1, True)

    @pl.loop(1, n_dest)
    def _(step):
        source = lax.rem(my_source + step, n_dest)
        pltpu.make_async_copy(landed.at[source], landed.at[source], out_recv.at[source]).wait()

    for source in range(n_dest):
        grown = landed[source].astype(jnp.float32)
        pieces = [grown[i * own_tokens:(i + 1) * own_tokens] for i in range(heads)]
        out_ref[:, source * half:(source + 1) * half] = jnp.concatenate(pieces, axis=1).astype(
            jnp.bfloat16
        )

    q_copy.wait_send()
    cross(0).wait_send()

    @pl.loop(1, direct)
    def _(step):
        same(step).wait_send()
        cross(step).wait_send()

    if relayed:
        for side in range(2):
            relay(side).wait_send()

    @pl.loop(1, n_dest)
    def _(step):
        send(lax.rem(mine + step, n_dest)).wait_send()


def per_device(n_ctx, n_head, queries, kv_cache, fill_len, prompt_offset):
    tokens, feats = queries.shape
    slots = kv_cache.shape[1]
    half = feats // 2
    n_dest = 2 * n_head
    own_tokens = tokens // n_head
    block = own_tokens * (half // HEAD_DIM)
    rows = n_dest * block
    slab = 2 * slots + FILL_ROWS
    bf16, f32 = jnp.bfloat16, jnp.float32
    dma = pltpu.SemaphoreType.DMA
    return pl.pallas_call(
        functools.partial(kernel, n_ctx, n_head),
        out_shape=jax.ShapeDtypeStruct((own_tokens, n_head * feats), bf16),
        in_specs=[
            pl.BlockSpec(memory_space=pltpu.HBM),
            pl.BlockSpec(memory_space=pltpu.HBM),
            pl.BlockSpec(memory_space=pltpu.HBM),
            pl.BlockSpec(memory_space=pltpu.HBM),
        ],
        out_specs=pl.BlockSpec(memory_space=pltpu.VMEM),
        scratch_shapes=[
            pltpu.VMEM((n_ctx, slab, HEAD_DIM), bf16),
            pltpu.VMEM((slab, HEAD_DIM), bf16),
            pltpu.VMEM((2, tokens, half), bf16),
            pltpu.VMEM((HEAD_DIM, rows), bf16),
            pltpu.VMEM((HEAD_DIM, rows), f32),
            pltpu.VMEM((1, rows), f32),
            pltpu.VMEM((1, rows), f32),
            pltpu.VMEM((n_dest, block, HEAD_DIM), bf16),
            pltpu.VMEM((n_dest, block, HEAD_DIM), bf16),
            pltpu.SMEM((1,), jnp.int32),
            pltpu.SMEM((1,), jnp.int32),
            dma((7,)), dma, dma, dma((n_ctx,)), dma((n_ctx,)), dma((n_dest,)), dma((n_dest,)),
        ],
        compiler_params=pltpu.CompilerParams(
            collective_id=0, has_side_effects=True, vmem_limit_bytes=63 * 2**20
        ),
    )(fill_len, prompt_offset, queries, kv_cache)


def solution(mesh):
    in_specs = (P("ctx", "head"), P(None, "ctx", "head"), P("ctx"), P())
    out_specs = P(("ctx", "head"), None)
    return jax.shard_map(
        functools.partial(per_device, mesh.shape["ctx"], mesh.shape["head"]),
        mesh=mesh, in_specs=in_specs, out_specs=out_specs, check_vma=False,
    )
```
